32 devices in a mesh: grp: 2 (over y), tblk: 4 (over x, core), inp: 4 (over z).
Axes of the slice: x: 2, y: 2, z: 4, core: 2. Of those that a mesh axis runs over, the one named last changes fastest.
Arguments:
- volt: bfloat16 [2, 192, 2, 512, 1024], P(None, 'grp', None, 'inp', 'tblk'), parts along dimension 1, may hold values from -20 to 20
- gains: float32 [2, 192, 512], P(None, ('grp', 'inp')), parts along dimension 1, may hold values from -0.25 to 0.25
- positions: float32 [3, 512], replicated, may hold values from -4 to 4
- directions: float32 [3, 256], replicated, may hold values from -1 to 1
- pattern: int32 [32, 64], replicated, may hold values 0 or 1
- dm_bins: int32 [256], replicated, may hold values from 0 to 31
- retention: float32 [256, 1024], P(None, 'tblk'), may hold values from 0.5 to 1
Outputs:
- detected: float32 [256, 192, 1024], P(None, ('grp', 'inp'), 'tblk'), parts along dimension 1
The draws below stay inside these ranges and needn't reach their ends.
There are 2 independent parts, one for each index of `grp`. The reference program is written for one: setup_inputs(seed, part) draws one part's arguments, and reference() takes and returns one part's arrays. A program takes and returns all parts, laid end to end along the dimension named above; an argument that names none is the same for every part. Nothing has to cross between parts.
All inputs are finite; a program needn't handle non-finite values.
Results may differ from the reference program's by a relative error of at most 0.0076.
Values may be sent and summed in bfloat16 or wider, within the bound.
A program may use at most 256 MiB of HBM per device.

```python
import math
import jax
import jax.numpy as jnp
from jax import lax

POL = 2
S = 512
C = 96
B = 256
L = 256
NDM = 32
BG = 32
SB = 64
SAMPLE_TOTAL = 1024


def draw_volt(key, part):
    key = jax.random.fold_in(key, 11)
    key_base, key_block = jax.random.split(key)
    shape = (POL, C, 2, S, SAMPLE_TOTAL)
    moment = jnp.arange(SAMPLE_TOTAL, dtype=jnp.float32) / SAMPLE_TOTAL
    base = jnp.clip(jax.random.normal(key_base, shape, jnp.float32), -8.0, 8.0)
    envelope = jnp.sqrt(1.0 + 2.0 * moment)
    factor = jnp.exp(jax.random.uniform(key_block, (SAMPLE_TOTAL // L,), jnp.float32, math.log(0.7), math.log(1.4)))
    envelope = envelope * jnp.repeat(factor, L)
    return (base * envelope).astype(jnp.bfloat16)


def draw_retention(key, part):
    key = jax.random.fold_in(key, 23)
    random_keys = jax.random.split(key, 7)
    share = 0.5
    quick = jax.random.uniform(random_keys[0], (B,), jnp.float32) < share
    quick_rate = jnp.exp(jax.random.uniform(random_keys[1], (B,), jnp.float32, math.log(1.0 / 50.0), math.log(1.0 / 30.0)))
    slow_rate = jnp.exp(jax.random.uniform(random_keys[2], (B,), jnp.float32, math.log(0.05), math.log(0.5))) / SAMPLE_TOTAL
    rate = jnp.where(quick, quick_rate, slow_rate)
    block_factor = jnp.exp(jax.random.uniform(random_keys[3], (B, SAMPLE_TOTAL // L), jnp.float32, math.log(0.6), math.log(1.5)))
    jitter = jnp.exp(jax.random.uniform(random_keys[4], (B, SAMPLE_TOTAL), jnp.float32, math.log(0.8), math.log(1.25)))
    factor = jnp.repeat(block_factor, L, axis=1) * jitter
    keeping = jnp.exp(-rate[:, None] * factor)
    pulse_events = jax.random.randint(random_keys[5], (3,), 0, SAMPLE_TOTAL)
    pulse_hit_mask = jnp.any(jnp.arange(SAMPLE_TOTAL, dtype=jnp.int32)[:, None] == pulse_events[None, :], axis=1)
    loss = jax.random.uniform(random_keys[6], (B, SAMPLE_TOTAL), jnp.float32, 0.6, 0.8)
    keeping = jnp.where(pulse_hit_mask[None, :], keeping * loss, keeping)
    return keeping.astype(jnp.float32)


def set_ends(entries, key, least, high):
    longest = entries.shape.index(max(entries.shape))
    spots = []
    for shift in (0, 1):
        where = [jax.random.randint(jax.random.fold_in(key, axis), (), 0, length) for axis, length in enumerate(entries.shape)]
        where[longest] = (where[longest] + shift) % entries.shape[longest]
        spots.append(tuple(where))
    return entries.at[spots[0]].set(least).at[spots[1]].set(high)


def block_scale(rng, dims, cuts, low, high):
    gain = 1.0
    for position, blocks in cuts:
        steps = jax.random.uniform(jax.random.fold_in(jax.random.fold_in(rng, 6), position), (blocks,), jnp.float32, low / len(cuts), high / len(cuts))
        gain = gain * jnp.repeat(jnp.exp(steps), dims[position] // blocks).reshape((-1,) + (1,) * (len(dims) - 1 - position))
    return gain


def gaussian(stream_key, dims, spread, most, cuts=(), kind=jnp.bfloat16):
    values = spread * jax.random.normal(stream_key, dims, jnp.float32)
    if cuts:
        values = values * block_scale(stream_key, dims, cuts, -0.22, 0.18)
    return jnp.clip(values, -most, most).astype(kind)


def setup_inputs(seed: int = 0, part: int = 0) -> dict:
    key_list = jax.random.split(jax.random.key(seed), 8)
    part_splits = jax.random.split(jax.random.fold_in(key_list[7], part), 8)
    return {
        "volt": draw_volt(jax.random.fold_in(jax.random.fold_in(key_list[7], part), 71), part),
        "gains": gaussian(part_splits[1], (2, C, S), S ** -0.5, 0.25, ((1, 4),), jnp.float32),
        "positions": jnp.clip(jax.random.uniform(key_list[2], (3, S), jnp.float32, -4.0, 4.0), -4.0, 4.0),
        "directions": jnp.clip(jax.random.uniform(key_list[3], (3, B), jnp.float32, -1.0, 1.0), -1.0, 1.0),
        "pattern": set_ends((jax.random.randint(key_list[4], (BG, SB), 0, 2) < 1).astype(jnp.int32), jax.random.fold_in(key_list[4], 1), 0, 1),
        "dm_bins": set_ends(jax.random.randint(key_list[5], (B,), 0, NDM), jax.random.fold_in(key_list[5], 1), 0, NDM - 1).astype(jnp.int32),
        "retention": draw_retention(jax.random.fold_in(key_list[7], 71), part),
    }


def beam_weights(gains, positions, directions, pattern, frequency):
    delay = directions[0][:, None] * positions[0][None, :] + directions[1][:, None] * positions[1][None, :] + directions[2][:, None] * positions[2][None, :]
    turning = (2.0 * math.pi) * frequency
    phase = turning[:, None, None] * delay[None, :, :]
    blocked = jnp.repeat(jnp.repeat(pattern, 8, axis=0), 8, axis=1).astype(jnp.float32)
    cosine = jnp.cos(phase)
    sine = jnp.sin(phase)
    real_part = blocked[None] * (gains[0][:, None, :] * cosine + gains[1][:, None, :] * sine)
    imag_part = blocked[None] * (gains[1][:, None, :] * cosine - gains[0][:, None, :] * sine)
    upper = jnp.concatenate([real_part, -imag_part], axis=-1)
    lower = jnp.concatenate([imag_part, real_part], axis=-1)
    return jnp.stack([upper, lower], axis=2).astype(jnp.bfloat16)


def transform_tables(length):
    extent = 2 * length
    indices = jnp.arange(extent, dtype=jnp.int32)
    product = (indices[:, None] * indices[None, :]) % extent
    angle = product.astype(jnp.float32) * (math.pi / length)
    cosine = jnp.cos(angle).astype(jnp.bfloat16)
    sine = jnp.sin(angle).astype(jnp.bfloat16)
    forward = jnp.concatenate([jnp.concatenate([cosine, -sine], axis=1), jnp.concatenate([sine, cosine], axis=1)], axis=0)
    inverse = jnp.concatenate([jnp.concatenate([cosine[:, length:], sine[:, length:]], axis=1), jnp.concatenate([-sine[:, length:], cosine[:, length:]], axis=1)], axis=0)
    return forward, inverse


def chirp_factors(dm_bins, frequency, length, bins_total):
    extent = 2 * length
    offsets = ((jnp.arange(extent, dtype=jnp.int32) + length) % extent - length).astype(jnp.float32) / extent
    measure = (dm_bins + 1).astype(jnp.float32) / bins_total
    angle = ((math.pi * length) * measure)[:, None, None] * (offsets * offsets)[None, None, :] / (frequency * frequency * frequency)[None, :, None]
    return jnp.cos(angle), jnp.sin(angle)


def dedisperse(series, forward, inverse, chirp_cos, chirp_sin):
    shape = series.shape
    length = shape[-1] // 2
    rows_flat = series.reshape(-1, 4 * length)
    spectrum = jnp.dot(rows_flat, forward, preferred_element_type=jnp.float32).reshape(shape)
    real_part = spectrum[:, :, :, 0]
    imag_part = spectrum[:, :, :, 1]
    turned_real = real_part * chirp_cos + imag_part * chirp_sin
    turned_imag = imag_part * chirp_cos - real_part * chirp_sin
    rotated_signal = jnp.stack([turned_real, turned_imag], axis=3).astype(jnp.bfloat16)
    signal = jnp.dot(rotated_signal.reshape(-1, 4 * length), inverse, preferred_element_type=jnp.float32) * (1.0 / (2 * length))
    signal = signal.reshape(shape[0], shape[1], shape[2], 2, length)
    return jnp.sum(signal * signal, axis=(0, 3))


def reference(volt, gains, positions, directions, pattern, dm_bins, retention):
    forward, inverse = transform_tables(L)
    blocks = SAMPLE_TOTAL // L

    def one_channel(channel):
        frequency = (1.0 + channel.astype(jnp.float32) / C).reshape(1)
        gain_slice = lax.dynamic_slice_in_dim(gains, channel, 1, axis=1)
        station_weights = beam_weights(gain_slice, positions, directions, pattern, frequency)
        samples = lax.dynamic_index_in_dim(volt, channel, axis=1, keepdims=False)
        samples = samples.reshape(POL, 2 * S, SAMPLE_TOTAL)
        beams = jnp.einsum('cbrs,psl->pbcrl', station_weights.astype(jnp.float32), samples.astype(jnp.float32)).astype(jnp.bfloat16)
        beams = beams.reshape(POL, B, 2, blocks, L)
        earlier = jnp.concatenate([jnp.zeros_like(beams[:, :, :, :1]), beams[:, :, :, :-1]], axis=3)
        series = jnp.concatenate([earlier, beams], axis=4)
        series = jnp.moveaxis(series, 3, 2)
        chirp_cos, chirp_sin = chirp_factors(dm_bins, frequency, L, NDM)
        power = dedisperse(series, forward, inverse, chirp_cos, chirp_sin).reshape(B, SAMPLE_TOTAL)

        def advance(state, inputs):
            level, weight = state
            current, keeping = inputs
            level = keeping * level + (1.0 - keeping) * current
            weight = keeping * weight + (1.0 - keeping)
            return (level, weight), current - level / weight

        start = (jnp.zeros((B,), jnp.float32), jnp.zeros((B,), jnp.float32))
        _, result = lax.scan(advance, start, (power.T, retention.T))
        return result.T

    stacked = lax.map(one_channel, jnp.arange(C, dtype=jnp.int32))
    return jnp.moveaxis(stacked, 0, 1)
```

```python
import functools
import math

import jax
import jax.numpy as jnp
import ml_dtypes
import numpy as np
from jax import lax
from jax.experimental import pallas as pl
from jax.experimental.pallas import tpu as pltpu
from jax.sharding import PartitionSpec as P

C = 96
NDM = 32
MESH = pl.DeviceIdType.MESH
WINDOW = 4
SLOTS = 4
LANES = 128


def transform_tables(length):
    extent = 2 * length
    indices = np.arange(extent, dtype=np.int64)
    angle = (indices[:, None] * indices[None, :] % extent) * (math.pi / length)
    cosine = np.cos(angle)
    sine = np.sin(angle)
    forward = np.block([[cosine, -sine], [sine, cosine]])
    inverse = np.block([[cosine[:, length:], sine[:, length:]], [-sine[:, length:], cosine[:, length:]]])
    narrow = lambda table: table.astype(np.float32).astype(ml_dtypes.bfloat16)
    return narrow(forward), narrow(inverse)


def cos_sin(x):
    turns = jnp.floor(x * (2.0 / math.pi) + 0.5)
    r = x - turns * 1.5703125
    r = r - turns * 4.837512969970703125e-4
    r = r - turns * 7.549789948768648e-8
    quarter = turns.astype(jnp.int32)
    z = r * r
    s = r + r * z * (-1.6666654611e-1 + z * (8.3321608736e-3 + z * -1.9515295891e-4))
    c = 1.0 - 0.5 * z + z * z * (4.166664568298827e-2 + z * (-1.388731625493765e-3 + z * 2.443315711809948e-5))
    swap = (quarter & 1) == 1
    cosine = jnp.where(swap, s, c)
    sine = jnp.where(swap, c, s)
    cosine = jnp.where(((quarter + 1) & 2) == 2, -cosine, cosine)
    sine = jnp.where((quarter & 2) == 2, -sine, sine)
    return cosine, sine


def kernel(
    n_inp, n_blk,
    volt, gains, positions, columns, pattern, retention, forward_hbm, inverse_hbm,
    partial, correction, entry,
    samples, previous, current, weights, delay, mask, chirp, turned, keep, inv_weight, cum,
    forward, inverse, out_buf, totals, decays,
    volt_send, volt_recv, own_sem, beam_send, beam_recv, out_sem, table_sem,
    total_send, total_recv, decay_send, decay_recv,
):
    here = gains.shape[1]
    stations = positions.shape[1]
    share = volt.shape[3]
    beams, length = retention.shape
    extent = 2 * length
    steps = keep.shape[0]
    z = lax.axis_index("inp")
    t = lax.axis_index("tblk")

    barrier = pltpu.get_barrier_semaphore()
    for s in range(1, n_inp):
        pl.semaphore_signal(barrier, inc=1, device_id={"inp": lax.rem(z + s, n_inp)}, device_id_type=MESH)
    for s in range(1, n_blk):
        pl.semaphore_signal(barrier, inc=1, device_id={"tblk": lax.rem(t + s, n_blk)}, device_id_type=MESH)
    pl.semaphore_wait(barrier, n_inp - 1 + n_blk - 1)

    def rows_of(device):
        return pl.ds(pl.multiple_of(device * share, share), share)

    def volt_out(j, s):
        to = lax.rem(z + s, n_inp)
        return pltpu.make_async_remote_copy(
            src_ref=volt.at[:, to * here + j],
            dst_ref=samples.at[j, :, :, rows_of(z)],
            send_sem=volt_send.at[j, s],
            recv_sem=volt_recv.at[j, s],
            device_id={"inp": to},
            device_id_type=MESH,
        )

    def volt_in(j, s):
        source = lax.rem(z + n_inp - s, n_inp)
        return pltpu.make_async_remote_copy(
            src_ref=volt.at[:, source * here + j],
            dst_ref=samples.at[j, :, :, rows_of(source)],
            send_sem=volt_send.at[j, s],
            recv_sem=volt_recv.at[j, s],
            device_id={"inp": source},
            device_id_type=MESH,
        )

    def volt_own(j):
        return pltpu.make_async_copy(volt.at[:, z * here + j], samples.at[j, :, :, rows_of(z)], own_sem.at[j])

    def beams_out(j):
        slot = lax.rem(j, SLOTS)
        return pltpu.make_async_remote_copy(
            src_ref=current.at[slot],
            dst_ref=previous.at[j],
            send_sem=beam_send.at[slot],
            recv_sem=beam_recv.at[j],
            device_id={"tblk": lax.rem(t + 1, n_blk)},
            device_id_type=MESH,
        )

    def result_out(j):
        slot = lax.rem(j, 2)
        return pltpu.make_async_copy(out_buf.at[slot], partial.at[j], out_sem.at[slot])

    def to_blocks(buffer, s, send, recv, source):
        return pltpu.make_async_remote_copy(
            src_ref=buffer.at[source],
            dst_ref=buffer.at[source],
            send_sem=send.at[s],
            recv_sem=recv.at[s],
            device_id={"tblk": lax.rem(t + s, n_blk)},
            device_id_type=MESH,
        )

    def send_channel(j):
        for s in range(1, n_inp):
            volt_out(j, s).start()
        volt_own(j).start()

    for j in range(min(WINDOW, here)):
        send_channel(j)

    tables = [
        pltpu.make_async_copy(forward_hbm, forward, table_sem.at[0]),
        pltpu.make_async_copy(inverse_hbm, inverse, table_sem.at[1]),
    ]
    for table in tables:
        table.start()

    delay[...] = (
        columns[:, 0:1] * positions[0:1, :]
        + columns[:, 1:2] * positions[1:2, :]
        + columns[:, 2:3] * positions[2:3, :]
    )
    groups, blocks = pattern.shape
    rise = lax.broadcasted_iota(jnp.int32, (beams, groups), 0) // (beams // groups)
    rise = (rise == lax.broadcasted_iota(jnp.int32, (beams, groups), 1)).astype(jnp.float32).astype(jnp.bfloat16)
    wide = lax.broadcasted_iota(jnp.int32, (blocks, stations), 1) // (stations // blocks)
    wide = (wide == lax.broadcasted_iota(jnp.int32, (blocks, stations), 0)).astype(jnp.float32).astype(jnp.bfloat16)
    cells = pattern[...].astype(jnp.float32).astype(jnp.bfloat16)
    spread = jnp.dot(rise, cells, preferred_element_type=jnp.float32).astype(jnp.bfloat16)
    mask[...] = jnp.dot(spread, wide, preferred_element_type=jnp.float32)

    moment = lax.broadcasted_iota(jnp.int32, (beams, length), 1)
    cum[...] = retention[...]
    inv_weight[...] = 1.0 - retention[...]
    for k in range(steps):
        reach = 1 << k
        product = cum[...]
        masked = jnp.where(moment >= reach, product, 0.0)
        keep[k] = masked
        inv_weight[...] += masked * pltpu.roll(inv_weight[...], reach, 1)
        cum[...] = product * jnp.where(moment >= reach, pltpu.roll(product, reach, 1), 1.0)
    lane = lax.broadcasted_iota(jnp.int32, (beams, LANES), 1)
    decays[t] = jnp.where(
        lane == 0,
        cum[:, length - 1 : length],
        inv_weight[:, length - 1 : length],
    )
    for s in range(1, n_blk):
        to_blocks(decays, s, decay_send, decay_recv, t).start()
    for s in range(1, n_blk):
        to_blocks(decays, s, decay_send, decay_recv, t).wait_send()
        to_blocks(decays, s, decay_send, decay_recv, lax.rem(t + n_blk - s, n_blk)).wait_recv()
    carried = jnp.zeros((beams, 1), jnp.float32)
    for i in range(n_blk - 1):
        longer = decays[i, :, 0:1] * carried + decays[i, :, 1:2]
        carried = jnp.where(i < t, longer, carried)
    inv_weight[...] = 1.0 / (inv_weight[...] + cum[...] * carried)
    correction[...] = cum[...] * inv_weight[...]
    totals[t] = jnp.zeros((beams, LANES), jnp.float32)
    for table in tables:
        table.wait()

    tile = 32

    def frequency_of(j, width):
        channel = lax.broadcasted_iota(jnp.int32, (1, width), 1) * 0 + (z * here + j)
        return 1.0 + channel.astype(jnp.float32) / C

    def make_weights(j):
        turning = (2.0 * math.pi) * frequency_of(j, stations)
        gain_real = gains[0, pl.ds(j, 1), :]
        gain_imag = gains[1, pl.ds(j, 1), :]

        @pl.loop(0, beams // tile)
        def _(i):
            rows = pl.ds(pl.multiple_of(i * tile, tile), tile)
            lower = pl.ds(pl.multiple_of(beams + i * tile, tile), tile)
            cosine, sine = cos_sin(turning * delay[rows, :])
            open_here = mask[rows, :]
            real = open_here * (gain_real * cosine + gain_imag * sine)
            imag = open_here * (gain_imag * cosine - gain_real * sine)
            weights[rows, 0:stations] = real.astype(jnp.bfloat16)
            weights[rows, stations:] = (-imag).astype(jnp.bfloat16)
            weights[lower, 0:stations] = imag.astype(jnp.bfloat16)
            weights[lower, stations:] = real.astype(jnp.bfloat16)

    def make_chirp(j):
        frequency = frequency_of(j, extent)
        index = lax.broadcasted_iota(jnp.int32, (1, extent), 1)
        offsets = jnp.where(index < length, index, index - extent).astype(jnp.float32) / extent
        shape = offsets * offsets / (frequency * frequency * frequency)

        @pl.loop(0, beams // tile)
        def _(i):
            rows = pl.ds(pl.multiple_of(i * tile, tile), tile)
            cosine, sine = cos_sin((math.pi * length) * columns[rows, 3:4] * shape)
            chirp[0, rows, :] = cosine
            chirp[1, rows, :] = sine

    @pl.loop(0, here + 1)
    def _(step):
        @pl.when(step < here)
        def _():
            j = step
            make_weights(j)
            for s in range(1, n_inp):
                volt_in(j, s).wait_recv()
            volt_own(j).wait()
            for s in range(1, n_inp):
                volt_out(j, s).wait_send()

            @pl.when(j + WINDOW < here)
            def _():
                send_channel(j + WINDOW)

            @pl.when(j >= SLOTS)
            def _():
                beams_out(j - SLOTS).wait_send()

            slot = lax.rem(j, SLOTS)
            for p in range(2):
                formed = jnp.dot(
                    weights[...],
                    samples[j, p].reshape(2 * stations, length),
                    preferred_element_type=jnp.float32,
                ).astype(jnp.bfloat16)
                current[slot, 0, p * beams : (p + 1) * beams] = formed[:beams]
                current[slot, 1, p * beams : (p + 1) * beams] = formed[beams:]
            beams_out(j).start()

        @pl.when(step >= 1)
        def _():
            j = step - 1
            make_chirp(j)
            beams_out(j).wait_recv()
            slot = lax.rem(j, SLOTS)
            first = t == 0
            power = jnp.zeros((beams, length), jnp.float32)
            for p in range(2):
                part = slice(p * beams, (p + 1) * beams)
                behind_real = previous[j, 0, part]
                behind_imag = previous[j, 1, part]
                nothing = jnp.zeros_like(behind_real)
                series = jnp.concatenate(
                    [
                        jnp.where(first, nothing, behind_real),
                        current[slot, 0, part],
                        jnp.where(first, nothing, behind_imag),
                        current[slot, 1, part],
                    ],
                    axis=1,
                )
                for k in range(2):
                    low, high = k * length, (k + 1) * length
                    real = jnp.dot(series, forward[:, low:high], preferred_element_type=jnp.float32)
                    imag = jnp.dot(
                        series, forward[:, extent + low : extent + high], preferred_element_type=jnp.float32
                    )
                    cosine = chirp[0, :, low:high]
                    sine = chirp[1, :, low:high]
                    turned[:, low:high] = (real * cosine + imag * sine).astype(jnp.bfloat16)
                    turned[:, extent + low : extent + high] = (imag * cosine - real * sine).astype(jnp.bfloat16)
                for half in range(2):
                    signal = jnp.dot(
                        turned[...],
                        inverse[:, half * length : (half + 1) * length],
                        preferred_element_type=jnp.float32,
                    ) * (1.0 / extent)
                    power += signal * signal

            level = (1.0 - retention[...]) * power
            for k in range(steps):
                level += keep[k] * pltpu.roll(level, 1 << k, 1)
            totals[t] = jnp.where(lane == j, level[:, length - 1 : length], totals[t])

            @pl.when(j >= 2)
            def _():
                result_out(j - 2).wait()

            out_buf[lax.rem(j, 2)] = power - level * inv_weight[...]
            result_out(j).start()

    for s in range(1, n_blk):
        to_blocks(totals, s, total_send, total_recv, t).start()
    for j in range(max(here - SLOTS, 0), here):
        beams_out(j).wait_send()
    for j in range(max(here - 2, 0), here):
        result_out(j).wait()
    for s in range(1, n_blk):
        to_blocks(totals, s, total_send, total_recv, t).wait_send()
        to_blocks(totals, s, total_send, total_recv, lax.rem(t + n_blk - s, n_blk)).wait_recv()
    carried = jnp.zeros((beams, LANES), jnp.float32)
    for i in range(n_blk - 1):
        longer = decays[i, :, 0:1] * carried + totals[i]
        carried = jnp.where(i < t, longer, carried)
    entry[...] = carried


def per_device(volt, gains, positions, directions, pattern, dm_bins, retention):
    n_inp, n_blk = lax.axis_size("inp"), lax.axis_size("tblk")
    here = gains.shape[1]
    stations = positions.shape[1]
    beams, length = retention.shape
    extent = 2 * length
    steps = (length - 1).bit_length()
    measure = (dm_bins + 1).astype(jnp.float32) / NDM
    columns = jnp.concatenate([directions, measure[None, :]], axis=0).T
    forward, inverse = transform_tables(length)
    inside = pl.BlockSpec(memory_space=pltpu.VMEM)
    outside = pl.BlockSpec(memory_space=pl.ANY)
    f32, bf16 = jnp.float32, jnp.bfloat16
    dma = pltpu.SemaphoreType.DMA
    partial, correction, entry = pl.pallas_call(
        functools.partial(kernel, n_inp, n_blk),
        out_shape=[
            jax.ShapeDtypeStruct((here, beams, length), f32),
            jax.ShapeDtypeStruct((beams, length), f32),
            jax.ShapeDtypeStruct((beams, LANES), f32),
        ],
        in_specs=[outside, inside, inside, inside, inside, inside, outside, outside],
        out_specs=[outside, inside, inside],
        scratch_shapes=[
            pltpu.VMEM((here, 2, 2, stations, length), bf16),
            pltpu.VMEM((here, 2, 2 * beams, length), bf16),
            pltpu.VMEM((SLOTS, 2, 2 * beams, length), bf16),
            pltpu.VMEM((2 * beams, 2 * stations), bf16),
            pltpu.VMEM((beams, stations), f32),
            pltpu.VMEM((beams, stations), f32),
            pltpu.VMEM((2, beams, extent), f32),
            pltpu.VMEM((beams, 2 * extent), bf16),
            pltpu.VMEM((steps, beams, length), f32),
            pltpu.VMEM((beams, length), f32),
            pltpu.VMEM((beams, length), f32),
            pltpu.VMEM((2 * extent, 2 * extent), bf16),
            pltpu.VMEM((2 * extent, extent), bf16),
            pltpu.VMEM((2, beams, length), f32),
            pltpu.VMEM((n_blk, beams, LANES), f32),
            pltpu.VMEM((n_blk, beams, LANES), f32),
            dma((here, n_inp)),
            dma((here, n_inp)),
            dma((here,)),
            dma((SLOTS,)),
            dma((here,)),
            dma((2,)),
            dma((2,)),
            dma((n_blk,)),
            dma((n_blk,)),
            dma((n_blk,)),
            dma((n_blk,)),
        ],
        compiler_params=pltpu.CompilerParams(
            collective_id=0, has_side_effects=True, vmem_limit_bytes=60 * 1024 * 1024
        ),
        cost_estimate=pl.CostEstimate(
            flops=2 * here * 2 * beams * (2 * stations * 2 * length + 2 * extent * 3 * extent),
            bytes_accessed=2 * volt.size + 4 * here * beams * length,
            transcendentals=0,
        ),
    )(volt, gains, positions, columns, pattern, retention, jnp.asarray(forward), jnp.asarray(inverse))
    late = correction[None] * entry[:, :here].T[:, :, None]
    return jnp.transpose(partial - late, (1, 0, 2))


def solution(mesh):
    placed = (
        P(None, "grp", None, "inp", "tblk"),
        P(None, ("grp", "inp"), None),
        P(),
        P(),
        P(),
        P(),
        P(None, "tblk"),
    )
    return jax.shard_map(
        per_device,
        mesh=mesh,
        in_specs=placed,
        out_specs=P(None, ("grp", "inp"), "tblk"),
        check_vma=False,
    )
```

```python
import functools
import math

import jax
import jax.numpy as jnp
import ml_dtypes
import numpy as np
from jax import lax
from jax.experimental import pallas as pl
from jax.experimental.pallas import tpu as pltpu
from jax.sharding import PartitionSpec as P

C = 96
NDM = 32
MESH = pl.DeviceIdType.MESH
WINDOW = 4
SLOTS = 4
LANES = 128


def transform_tables(length):
    extent = 2 * length
    indices = np.arange(extent, dtype=np.int64)
    angle = (indices[:, None] * indices[None, :] % extent) * (math.pi / length)
    cosine = np.cos(angle)
    sine = np.sin(angle)
    forward = np.block([[cosine, -sine], [sine, cosine]])
    inverse = np.block([[cosine[:, length:], sine[:, length:]], [-sine[:, length:], cosine[:, length:]]])
    narrow = lambda table: table.astype(np.float32).astype(ml_dtypes.bfloat16)
    return narrow(forward), narrow(inverse)


def cos_sin(x):
    turns = jnp.floor(x * (2.0 / math.pi) + 0.5)
    r = x - turns * 1.5703125
    r = r - turns * 4.837512969970703125e-4
    r = r - turns * 7.549789948768648e-8
    quarter = turns.astype(jnp.int32)
    z = r * r
    s = r + r * z * (-1.6666654611e-1 + z * (8.3321608736e-3 + z * -1.9515295891e-4))
    c = 1.0 - 0.5 * z + z * z * (4.166664568298827e-2 + z * (-1.388731625493765e-3 + z * 2.443315711809948e-5))
    swap = (quarter & 1) == 1
    cosine = jnp.where(swap, s, c)
    sine = jnp.where(swap, c, s)
    cosine = jnp.where(((quarter + 1) & 2) == 2, -cosine, cosine)
    sine = jnp.where((quarter & 2) == 2, -sine, sine)
    return cosine, sine


def kernel(
    n_inp, n_blk,
    volt, gains, positions, columns, pattern, retention, forward_hbm, inverse_hbm,
    partial, correction, entry,
    samples, previous, current, weights, delay, mask, chirp, turned, keep, inv_weight, cum,
    forward, inverse, out_buf, ends, totals, decays, decay_rows,
    volt_send, volt_recv, own_sem, beam_send, beam_recv, out_sem, table_sem,
    total_send, total_recv, decay_send, decay_recv,
):
    here = gains.shape[1]
    stations = positions.shape[1]
    share = volt.shape[3]
    beams, length = retention.shape
    extent = 2 * length
    steps = keep.shape[0]
    bunch = out_buf.shape[2]
    held = totals.shape[1]
    z = lax.axis_index("inp")
    t = lax.axis_index("tblk")

    barrier = pltpu.get_barrier_semaphore()
    for s in range(1, n_inp):
        pl.semaphore_signal(barrier, inc=1, device_id={"inp": lax.rem(z + s, n_inp)}, device_id_type=MESH)
    for s in range(1, n_blk):
        pl.semaphore_signal(barrier, inc=1, device_id={"tblk": lax.rem(t + s, n_blk)}, device_id_type=MESH)
    pl.semaphore_wait(barrier, n_inp - 1 + n_blk - 1)

    def rows_of(device):
        return pl.ds(pl.multiple_of(device * share, share), share)

    def volt_out(j, s):
        to = lax.rem(z + s, n_inp)
        return pltpu.make_async_remote_copy(
            src_ref=volt.at[:, to * here + j],
            dst_ref=samples.at[j, :, :, rows_of(z)],
            send_sem=volt_send.at[j, s],
            recv_sem=volt_recv.at[j, s],
            device_id={"inp": to},
            device_id_type=MESH,
        )

    def volt_in(j, s):
        source = lax.rem(z + n_inp - s, n_inp)
        return pltpu.make_async_remote_copy(
            src_ref=volt.at[:, source * here + j],
            dst_ref=samples.at[j, :, :, rows_of(source)],
            send_sem=volt_send.at[j, s],
            recv_sem=volt_recv.at[j, s],
            device_id={"inp": source},
            device_id_type=MESH,
        )

    def volt_own(j):
        return pltpu.make_async_copy(volt.at[:, z * here + j], samples.at[j, :, :, rows_of(z)], own_sem.at[j])

    def beams_out(j):
        slot = lax.rem(j, SLOTS)
        return pltpu.make_async_remote_copy(
            src_ref=current.at[slot],
            dst_ref=previous.at[j],
            send_sem=beam_send.at[slot],
            recv_sem=beam_recv.at[j],
            device_id={"tblk": lax.rem(t + 1, n_blk)},
            device_id_type=MESH,
        )

    def result_out(j):
        group = j // bunch
        slot = lax.rem(group, 2)
        return pltpu.make_async_copy(
            out_buf.at[slot],
            partial.at[:, pl.ds(pl.multiple_of(group * bunch, bunch), bunch)],
            out_sem.at[slot],
        )

    def to_blocks(buffer, s, send, recv, source):
        return pltpu.make_async_remote_copy(
            src_ref=buffer.at[source],
            dst_ref=buffer.at[source],
            send_sem=send.at[s],
            recv_sem=recv.at[s],
            device_id={"tblk": lax.rem(t + s, n_blk)},
            device_id_type=MESH,
        )

    def send_channel(j):
        for s in range(1, n_inp):
            volt_out(j, s).start()
        volt_own(j).start()

    for j in range(min(WINDOW, here)):
        send_channel(j)

    tables = [
        pltpu.make_async_copy(forward_hbm, forward, table_sem.at[0]),
        pltpu.make_async_copy(inverse_hbm, inverse, table_sem.at[1]),
    ]
    for table in tables:
        table.start()

    delay[...] = (
        columns[:, 0:1] * positions[0:1, :]
        + columns[:, 1:2] * positions[1:2, :]
        + columns[:, 2:3] * positions[2:3, :]
    )
    groups, blocks = pattern.shape
    rise = lax.broadcasted_iota(jnp.int32, (beams, groups), 0) // (beams // groups)
    rise = (rise == lax.broadcasted_iota(jnp.int32, (beams, groups), 1)).astype(jnp.float32).astype(jnp.bfloat16)
    wide = lax.broadcasted_iota(jnp.int32, (blocks, stations), 1) // (stations // blocks)
    wide = (wide == lax.broadcasted_iota(jnp.int32, (blocks, stations), 0)).astype(jnp.float32).astype(jnp.bfloat16)
    cells = pattern[...].astype(jnp.float32).astype(jnp.bfloat16)
    spread = jnp.dot(rise, cells, preferred_element_type=jnp.float32).astype(jnp.bfloat16)
    mask[...] = jnp.dot(spread, wide, preferred_element_type=jnp.float32)

    moment = lax.broadcasted_iota(jnp.int32, (beams, length), 1)
    cum[...] = retention[...]
    inv_weight[...] = 1.0 - retention[...]
    for k in range(steps):
        reach = 1 << k
        product = cum[...]
        masked = jnp.where(moment >= reach, product, 0.0)
        keep[k] = masked
        inv_weight[...] += masked * pltpu.roll(inv_weight[...], reach, 1)
        cum[...] = product * jnp.where(moment >= reach, pltpu.roll(product, reach, 1), 1.0)
    lane = lax.broadcasted_iota(jnp.int32, (beams, LANES), 1)
    decays[t] = jnp.where(
        lane == 0,
        cum[:, length - 1 : length],
        inv_weight[:, length - 1 : length],
    )
    for s in range(1, n_blk):
        to_blocks(decays, s, decay_send, decay_recv, t).start()
    for s in range(1, n_blk):
        to_blocks(decays, s, decay_send, decay_recv, t).wait_send()
        to_blocks(decays, s, decay_send, decay_recv, lax.rem(t + n_blk - s, n_blk)).wait_recv()
    carried = jnp.zeros((beams, 1), jnp.float32)
    for i in range(n_blk - 1):
        longer = decays[i, :, 0:1] * carried + decays[i, :, 1:2]
        carried = jnp.where(i < t, longer, carried)
    inv_weight[...] = 1.0 / (inv_weight[...] + cum[...] * carried)
    correction[...] = cum[...] * inv_weight[...]
    ends[...] = jnp.zeros((beams, LANES), jnp.float32)
    for i in range(n_blk - 1):
        decay_rows[i] = jnp.transpose(decays[i])[0:8]
    for table in tables:
        table.wait()

    tile = 32

    def frequency_of(j, width):
        channel = lax.broadcasted_iota(jnp.int32, (1, width), 1) * 0 + (z * here + j)
        return 1.0 + channel.astype(jnp.float32) / C

    def make_weights(j):
        turning = (2.0 * math.pi) * frequency_of(j, stations)
        gain_real = gains[0, pl.ds(j, 1), :]
        gain_imag = gains[1, pl.ds(j, 1), :]

        @pl.loop(0, beams // tile)
        def _(i):
            rows = pl.ds(pl.multiple_of(i * tile, tile), tile)
            lower = pl.ds(pl.multiple_of(beams + i * tile, tile), tile)
            cosine, sine = cos_sin(turning * delay[rows, :])
            open_here = mask[rows, :]
            real = open_here * (gain_real * cosine + gain_imag * sine)
            imag = open_here * (gain_imag * cosine - gain_real * sine)
            weights[rows, 0:stations] = real.astype(jnp.bfloat16)
            weights[rows, stations:] = (-imag).astype(jnp.bfloat16)
            weights[lower, 0:stations] = imag.astype(jnp.bfloat16)
            weights[lower, stations:] = real.astype(jnp.bfloat16)

    def make_chirp(j):
        frequency = frequency_of(j, extent)
        index = lax.broadcasted_iota(jnp.int32, (1, extent), 1)
        offsets = jnp.where(index < length, index, index - extent).astype(jnp.float32) / extent
        shape = offsets * offsets / (frequency * frequency * frequency)

        @pl.loop(0, beams // tile)
        def _(i):
            rows = pl.ds(pl.multiple_of(i * tile, tile), tile)
            cosine, sine = cos_sin((math.pi * length) * columns[rows, 3:4] * shape)
            chirp[0, rows, :] = cosine
            chirp[1, rows, :] = sine

    @pl.loop(0, here + 1)
    def _(step):
        @pl.when(step < here)
        def _():
            j = step
            make_weights(j)
            for s in range(1, n_inp):
                volt_in(j, s).wait_recv()
            volt_own(j).wait()
            for s in range(1, n_inp):
                volt_out(j, s).wait_send()

            @pl.when(j + WINDOW < here)
            def _():
                send_channel(j + WINDOW)

            @pl.when(j >= SLOTS)
            def _():
                beams_out(j - SLOTS).wait_send()

            slot = lax.rem(j, SLOTS)
            for p in range(2):
                formed = jnp.dot(
                    weights[...],
                    samples[j, p].reshape(2 * stations, length),
                    preferred_element_type=jnp.float32,
                ).astype(jnp.bfloat16)
                current[slot, 0, p * beams : (p + 1) * beams] = formed[:beams]
                current[slot, 1, p * beams : (p + 1) * beams] = formed[beams:]
            beams_out(j).start()

        @pl.when(step >= 1)
        def _():
            j = step - 1
            make_chirp(j)
            beams_out(j).wait_recv()
            slot = lax.rem(j, SLOTS)
            first = t == 0
            power = jnp.zeros((beams, length), jnp.float32)
            for p in range(2):
                part = slice(p * beams, (p + 1) * beams)
                behind_real = previous[j, 0, part]
                behind_imag = previous[j, 1, part]
                nothing = jnp.zeros_like(behind_real)
                series = jnp.concatenate(
                    [
                        jnp.where(first, nothing, behind_real),
                        current[slot, 0, part],
                        jnp.where(first, nothing, behind_imag),
                        current[slot, 1, part],
                    ],
                    axis=1,
                )
                for k in range(2):
                    low, high = k * length, (k + 1) * length
                    real = jnp.dot(series, forward[:, low:high], preferred_element_type=jnp.float32)
                    imag = jnp.dot(
                        series, forward[:, extent + low : extent + high], preferred_element_type=jnp.float32
                    )
                    cosine = chirp[0, :, low:high]
                    sine = chirp[1, :, low:high]
                    turned[:, low:high] = (real * cosine + imag * sine).astype(jnp.bfloat16)
                    turned[:, extent + low : extent + high] = (imag * cosine - real * sine).astype(jnp.bfloat16)
                for half in range(2):
                    signal = jnp.dot(
                        turned[...],
                        inverse[:, half * length : (half + 1) * length],
                        preferred_element_type=jnp.float32,
                    ) * (1.0 / extent)
                    power += signal * signal

            level = (1.0 - retention[...]) * power
            for k in range(steps):
                level += keep[k] * pltpu.roll(level, 1 << k, 1)
            ends[...] = jnp.where(lane == j, level[:, length - 1 : length], ends[...])

            @pl.when((lax.rem(j, bunch) == 0) & (j >= 2 * bunch))
            def _():
                result_out(j - 2 * bunch).wait()

            out_buf[lax.rem(j // bunch, 2), :, lax.rem(j, bunch), :] = power - level * inv_weight[...]

            @pl.when(lax.rem(j, bunch) == bunch - 1)
            def _():
                result_out(j).start()

    totals[t] = jnp.transpose(ends[...])[0:held]
    for s in range(1, n_blk):
        to_blocks(totals, s, total_send, total_recv, t).start()
    for j in range(max(here - SLOTS, 0), here):
        beams_out(j).wait_send()
    for group in range(max(here // bunch - 2, 0), here // bunch):
        result_out(group * bunch).wait()
    for s in range(1, n_blk):
        to_blocks(totals, s, total_send, total_recv, t).wait_send()
        to_blocks(totals, s, total_send, total_recv, lax.rem(t + n_blk - s, n_blk)).wait_recv()
    carried = jnp.zeros((held, beams), jnp.float32)
    for i in range(n_blk - 1):
        longer = decay_rows[i, 0:1, :] * carried + totals[i]
        carried = jnp.where(i < t, longer, carried)
    entry[...] = carried


def per_device(volt, gains, positions, directions, pattern, dm_bins, retention):
    n_inp, n_blk = lax.axis_size("inp"), lax.axis_size("tblk")
    here = gains.shape[1]
    stations = positions.shape[1]
    beams, length = retention.shape
    extent = 2 * length
    steps = (length - 1).bit_length()
    bunch = 8 if here % 8 == 0 else here
    held = -(-here // 8) * 8
    measure = (dm_bins + 1).astype(jnp.float32) / NDM
    columns = jnp.concatenate([directions, measure[None, :]], axis=0).T
    forward, inverse = transform_tables(length)
    inside = pl.BlockSpec(memory_space=pltpu.VMEM)
    outside = pl.BlockSpec(memory_space=pl.ANY)
    f32, bf16 = jnp.float32, jnp.bfloat16
    dma = pltpu.SemaphoreType.DMA
    partial, correction, entry = pl.pallas_call(
        functools.partial(kernel, n_inp, n_blk),
        out_shape=[
            jax.ShapeDtypeStruct((beams, here, length), f32),
            jax.ShapeDtypeStruct((beams, length), f32),
            jax.ShapeDtypeStruct((held, beams), f32),
        ],
        in_specs=[outside, inside, inside, inside, inside, inside, outside, outside],
        out_specs=[outside, inside, inside],
        scratch_shapes=[
            pltpu.VMEM((here, 2, 2, stations, length), bf16),
            pltpu.VMEM((here, 2, 2 * beams, length), bf16),
            pltpu.VMEM((SLOTS, 2, 2 * beams, length), bf16),
            pltpu.VMEM((2 * beams, 2 * stations), bf16),
            pltpu.VMEM((beams, stations), f32),
            pltpu.VMEM((beams, stations), f32),
            pltpu.VMEM((2, beams, extent), f32),
            pltpu.VMEM((beams, 2 * extent), bf16),
            pltpu.VMEM((steps, beams, length), f32),
            pltpu.VMEM((beams, length), f32),
            pltpu.VMEM((beams, length), f32),
            pltpu.VMEM((2 * extent, 2 * extent), bf16),
            pltpu.VMEM((2 * extent, extent), bf16),
            pltpu.VMEM((2, beams, bunch, length), f32),
            pltpu.VMEM((beams, LANES), f32),
            pltpu.VMEM((n_blk, held, beams), f32),
            pltpu.VMEM((n_blk, beams, LANES), f32),
            pltpu.VMEM((n_blk, 8, beams), f32),
            dma((here, n_inp)),
            dma((here, n_inp)),
            dma((here,)),
            dma((SLOTS,)),
            dma((here,)),
            dma((2,)),
            dma((2,)),
            dma((n_blk,)),
            dma((n_blk,)),
            dma((n_blk,)),
            dma((n_blk,)),
        ],
        compiler_params=pltpu.CompilerParams(
            collective_id=0, has_side_effects=True, vmem_limit_bytes=60 * 1024 * 1024
        ),
        cost_estimate=pl.CostEstimate(
            flops=2 * here * 2 * beams * (2 * stations * 2 * length + 2 * extent * 3 * extent),
            bytes_accessed=2 * volt.size + 4 * here * beams * length,
            transcendentals=0,
        ),
    )(volt, gains, positions, columns, pattern, retention, jnp.asarray(forward), jnp.asarray(inverse))
    return partial - correction[:, None, :] * entry[:here].T[:, :, None]


def solution(mesh):
    placed = (
        P(None, "grp", None, "inp", "tblk"),
        P(None, ("grp", "inp"), None),
        P(),
        P(),
        P(),
        P(),
        P(None, "tblk"),
    )
    return jax.shard_map(
        per_device,
        mesh=mesh,
        in_specs=placed,
        out_specs=P(None, ("grp", "inp"), "tblk"),
        check_vma=False,
    )
```
